32 devices in a mesh: groups: 1, pool: 32 (over z, y, x, core).
Axes of the slice: x: 2, y: 2, z: 4, core: 2. Of those that a mesh axis runs over, the one named last changes fastest.
Arguments:
- tokens: bfloat16 [2048, 7168], P(('groups', 'pool')), may hold values from -6 to 6
- slot_ids: int32 [2048, 2], P(('groups', 'pool')), may hold values from 0 to 3, all different within a row; in each aligned block of 64 rows (0 to 63, 64 to 127, ...) at most 48 rows name the same one
- gate_codes: int32 [2048, 2], P(('groups', 'pool')), may hold values from 1 to 1024
- gate_up: bfloat16 [28672, 2048], P('pool'), may hold values from -0.0625 to 0.0625
- down_proj: bfloat16 [1024, 28672], P(None, 'pool'), may hold values from -0.1875 to 0.1875
Outputs:
- mixed: bfloat16 [2048, 7168], P(('groups', 'pool'))
The draws below stay inside these ranges and needn't reach their ends.
Inputs may be any that keep to these rules, and one draw needn't show every extreme that they name: `slot_ids`: each token names 2 different slots. Of the 64 tokens of one device, at most 48 name any one slot, and in every draw some slot is named by exactly 48 tokens of some device.
All inputs are finite; a program needn't handle non-finite values.
Results may differ from the reference program's by a relative error of at most 0.0058.
Values may be sent and summed in bfloat16 or wider, within the bound.
A program may use at most 128 MiB of HBM per device.

```python
import math
import jax
import jax.numpy as jnp
import numpy as np
from jax import lax

D = 7168
FFW = 1024
TOPK = 2
TOK_DEV = 64
SLOTS = 4
CAP = 48
TOKENS = 2048
N_POOL = 32


def with_ends(values, stream_key, smallest, largest):
    longest = values.shape.index(max(values.shape))
    spots = []
    for shift in (0, 1):
        where = [jax.random.randint(jax.random.fold_in(stream_key, axis), (), 0, length) for axis, length in enumerate(values.shape)]
        where[longest] = (where[longest] + shift) % values.shape[longest]
        spots.append(tuple(where))
    return values.at[spots[0]].set(smallest).at[spots[1]].set(largest)


def steps_of(own_key, extent, pieces, low, top_value):
    level = 1.0
    for dim, parts in pieces:
        draws = jax.random.uniform(jax.random.fold_in(jax.random.fold_in(own_key, 6), dim), (parts,), jnp.float32, low / len(pieces), top_value / len(pieces))
        level = level * jnp.repeat(jnp.exp(draws), extent[dim] // parts).reshape((-1,) + (1,) * (len(extent) - 1 - dim))
    return level


def deal_out(own_key, own, number, rows, number_of, top, most, slope):
    sequence = jax.random.permutation(own_key, number_of)
    heavy_load, common = load_shares(number_of, rows * top, most, slope, True), load_shares(number_of, rows * top, most, slope, False)
    places = jnp.arange(number_of)

    def named(lengths, offset_by):
        used = int((lengths > 0).sum())
        fixed = max(1, used // 4)
        moved = fixed + (places - fixed + offset_by * (used - fixed)) % max(1, number_of - fixed)
        return jnp.zeros((number_of,), jnp.int32).at[sequence[jnp.where(places < fixed, places, moved)]].set(jnp.asarray(lengths, jnp.int32))

    lengths = jnp.where(number % 4 == 0, named(heavy_load, number // 4), named(common, number - number // 4 - 1))
    mixed = jax.random.permutation(jax.random.fold_in(own, 3), number_of)
    giver, receiver = mixed[0:number_of // 2 * 2:2], mixed[1:number_of // 2 * 2:2]
    slack = jnp.minimum(lengths[giver] - 1, most - lengths[receiver]) // 2
    slack = jnp.where((giver == sequence[0]) | (receiver == sequence[0]) | (lengths[receiver] == 0), 0, jnp.maximum(slack, 0))
    moved = jax.random.randint(jax.random.fold_in(own, 4), (number_of // 2,), 0, 1 << 20) % (slack + 1)
    lengths = lengths.at[giver].add(-moved).at[receiver].add(moved)
    members = jnp.searchsorted(jnp.cumsum(lengths), jnp.arange(rows * top), side="right").astype(jnp.int32)
    grid = members.reshape(top, rows).T
    grid = grid[jax.random.permutation(jax.random.fold_in(own, 1), rows)]
    offset_by = jax.random.randint(jax.random.fold_in(own, 2), (rows, 1), 0, top)
    return jnp.take_along_axis(grid, (jnp.arange(top)[None, :] + offset_by) % top, axis=1)


def load_shares(amount, total, reach, skew, full):
    weights = [(1 << 20) // math.isqrt(rank ** skew) + 1 for rank in range(1, amount + 1)]
    largest = reach if full else min(reach, max(-(-total // amount), total * weights[0] // sum(weights)))
    least = 1 if total - largest >= amount - 1 else 0
    holding, spare = [largest] + [least] * (amount - 1), total - largest - least * (amount - 1)
    while spare > 0:
        candidates = [i for i in range(1, amount) if holding[i] < largest] or [i for i in range(1, amount) if holding[i] < reach]
        whole, budget = sum([weights[i] for i in candidates]), spare
        for i in candidates:
            extra = min(reach - holding[i], max(1, budget * weights[i] // whole), spare)
            holding[i] = holding[i] + extra
            spare = spare - extra
    return np.array(holding)


def scatter_about(rng, dims, scale, reach, shards=(), held_as=jnp.bfloat16):
    array = scale * jax.random.normal(rng, dims, jnp.float32)
    if shards:
        array = array * steps_of(rng, dims, shards, -0.22, 0.18)
    return jnp.clip(array, -reach, reach).astype(held_as)


def setup_inputs(seed: int = 0, part: int = 0) -> dict:
    key_of = jax.random.split(jax.random.key(seed), 6)
    own_keys = jax.random.split(jax.random.fold_in(key_of[5], part), 6)
    tokens = scatter_about(own_keys[0], (TOKENS, D), 1.0, 6.0, ((0, 32),))
    slot_ids_keys = jax.random.split(jax.random.fold_in(own_keys[1], 1), TOKENS // TOK_DEV)
    slot_ids_turns = jax.random.permutation(jax.random.fold_in(own_keys[1], 3), TOKENS // TOK_DEV)
    slot_ids = jax.vmap(lambda own, number: deal_out(jax.random.fold_in(own_keys[1], 2), own, number, TOK_DEV, SLOTS, TOPK, CAP, 2))(slot_ids_keys, slot_ids_turns).reshape((TOKENS, TOPK))
    gate_codes = with_ends(jax.random.randint(own_keys[2], (TOKENS, TOPK), 1, 1025), jax.random.fold_in(own_keys[2], 1), 1, 1024).astype(jnp.int32)
    gate_up = scatter_about(key_of[3], (SLOTS * D, 2 * FFW), D ** -0.5, 0.0625, ((0, 32),))
    down_proj = scatter_about(key_of[4], (FFW, SLOTS * D), FFW ** -0.5, 0.1875, ((1, 32),))
    return {"tokens": tokens, "slot_ids": slot_ids, "gate_codes": gate_codes, "gate_up": gate_up, "down_proj": down_proj}


def reference(tokens, slot_ids, gate_codes, gate_up, down_proj):
    rows_most = N_POOL * CAP
    weight = gate_codes.astype(jnp.float32) / 1024.0

    def one_slot(total, slot):
        named = slot_ids == slot
        taken = jnp.any(named, axis=1)
        share = jnp.sum(jnp.where(named, weight, 0.0), axis=1)
        order = jnp.argsort(jnp.logical_not(taken).astype(jnp.int32), stable=True)[:rows_most].astype(jnp.int32)
        rows = jnp.take(tokens, order, axis=0)
        start = (slot * D).astype(jnp.int32)
        w_gate_up = lax.dynamic_slice_in_dim(gate_up, start, D, 0)
        w_down = lax.dynamic_slice_in_dim(down_proj, start, D, 1)
        pre = jnp.dot(rows, w_gate_up, preferred_element_type=jnp.float32)
        hidden = (jax.nn.silu(pre[:, :FFW]) * pre[:, FFW:]).astype(jnp.bfloat16)
        expert_out = jnp.dot(hidden, w_down, preferred_element_type=jnp.float32).astype(jnp.bfloat16)
        scale = jnp.take(share, order)
        total = total.at[order].add(scale[:, None] * expert_out.astype(jnp.float32))
        return total, None

    total, _ = lax.scan(one_slot, jnp.zeros((TOKENS, D), jnp.float32), jnp.arange(SLOTS, dtype=jnp.int32))
    return total.astype(jnp.bfloat16)
```

```python
import jax
import jax.numpy as jnp
from jax import lax
from jax.sharding import PartitionSpec as P

SPAN = 8
BF = jnp.bfloat16
F32 = jnp.float32


def swap(value, mask):
    pairs = [(source, source ^ mask) for source in range(lax.axis_size("pool"))]
    return lax.ppermute(value, "pool", pairs)


def kept(value, side, axis):
    return lax.dynamic_index_in_dim(value, side, axis, keepdims=False)


def joined(mine, other, side, axis):
    return jnp.where(side == 1, jnp.stack([other, mine], axis), jnp.stack([mine, other], axis))


def reduce_rows(partial, core, x, y):
    half = partial.shape[-1] // 2
    grid = partial.reshape(2, 2, 2, -1, 2 * half)
    now = kept(grid, core, 0) + swap(kept(grid, 1 - core, 0).astype(BF), 1)
    first, second = now[..., :half], now[..., half:]
    first_in = swap(kept(first, 1 - x, 0).astype(BF), 2)
    second_in = swap(kept(second, 1 - y, 1).astype(BF), 4)
    first = kept(first, x, 0) + first_in
    second = kept(second, y, 1) + second_in
    first_in = swap(kept(first, 1 - y, 0).astype(BF), 4)
    second_in = swap(kept(second, 1 - x, 0).astype(BF), 2)
    return kept(first, y, 0) + first_in, kept(second, x, 0) + second_in


def gather_rows(hidden, core, x, y):
    half = hidden.shape[-1] // 2
    first, second = hidden[:, :half], hidden[:, half:]
    first_in, second_in = swap(first, 4), swap(second, 2)
    first = joined(first, first_in, y, 0)
    second = joined(second, second_in, x, 0)
    first_in, second_in = swap(first, 2), swap(second, 4)
    first = joined(first, first_in, x, 0)
    second = joined(second, second_in, y, 1)
    both = jnp.concatenate([first, second], axis=-1)
    both = joined(both, swap(both, 1), core, 0)
    return both.reshape(-1, 2 * half)


def on_device(tokens, slot_ids, gate_codes, gate_up, down_proj):
    pool_size = lax.axis_size("pool")
    slots = pool_size // SPAN
    tok_rows, width = tokens.shape
    topk = slot_ids.shape[1]
    piece = width // SPAN
    hidden_units = down_proj.shape[0]
    capacity = min(tok_rows, 3 * tok_rows * topk // (2 * slots))
    index = lax.axis_index("pool")
    member, own_slot = index % SPAN, index // SPAN
    core, x, y = member & 1, member >> 1 & 1, member >> 2 & 1
    planes = [[s * SPAN + m for m in range(SPAN)] for s in range(slots)]

    routing = jnp.concatenate([slot_ids, gate_codes], axis=1)
    routing = lax.all_gather(routing, "pool", axis_index_groups=planes)
    plane_slots, plane_codes = routing[..., :topk], routing[..., topk:]
    pieces = tokens.reshape(tok_rows, SPAN, piece).transpose(1, 0, 2)
    plane_tokens = lax.all_to_all(pieces, "pool", split_axis=0, concat_axis=0, axis_index_groups=planes, tiled=True)

    def routes(slot):
        named = plane_slots == slot
        taken = jnp.any(named, axis=2)
        place = jnp.cumsum(taken.astype(jnp.int32), axis=1) - 1
        code = jnp.sum(jnp.where(named, plane_codes, 0), axis=2)
        hot = (place[:, :, None] == jnp.arange(capacity)) & taken[:, :, None]
        return hot, code

    blocks, mixers = [], []
    for step in range(slots):
        hot, code = routes(own_slot ^ step)
        high = jnp.where(hot, (code // 32)[:, :, None], 0).astype(F32) / 32.0
        low = jnp.where(hot, (code % 32)[:, :, None], 0).astype(F32) / 1024.0
        mixers.append((high.astype(BF), low.astype(BF)))
        block = jnp.einsum("jtc,jtd->jcd", hot.astype(BF), plane_tokens, preferred_element_type=F32)
        blocks.append(block.astype(BF).reshape(SPAN * capacity, piece))

    order = [0] + list(reversed(range(1, slots)))
    arrived = {step: swap(blocks[step], step * SPAN) if step else blocks[step] for step in order}
    mixed = jnp.zeros((SPAN, tok_rows, piece), F32)
    for step in order:
        partial = jnp.dot(arrived[step], gate_up, preferred_element_type=F32)
        gate, up = reduce_rows(partial, core, x, y)
        hidden = gather_rows((jax.nn.silu(gate) * up).astype(BF), core, x, y)
        result = jnp.dot(hidden, down_proj, preferred_element_type=F32).astype(BF)
        back = (swap(result, step * SPAN) if step else result).reshape(SPAN, capacity, piece)
        for part in mixers[step]:
            mixed = mixed + jnp.einsum("jtc,jcd->jtd", part, back, preferred_element_type=F32)
    out = lax.all_to_all(mixed.astype(BF), "pool", split_axis=0, concat_axis=0, axis_index_groups=planes, tiled=True)
    return out.transpose(1, 0, 2).reshape(tok_rows, width)


def solution(mesh):
    rows = P(("groups", "pool"), None)
    return jax.shard_map(
        on_device,
        mesh=mesh,
        in_specs=(rows, rows, rows, P("pool", None), P(None, "pool")),
        out_specs=rows,
        check_vma=False,
    )
```

```python
import functools
import jax
import jax.numpy as jnp
from jax import lax
from jax.experimental import pallas as pl
from jax.experimental.pallas import tpu as pltpu
from jax.sharding import PartitionSpec as P

SPAN = 8
BF = jnp.bfloat16
F32 = jnp.float32


def swap(value, mask):
    pairs = [(source, source ^ mask) for source in range(lax.axis_size("pool"))]
    return lax.ppermute(value, "pool", pairs)


def at(index, rows):
    return pl.ds(pl.multiple_of(index * rows, 16), rows)


def expert_kernel(cap, rows_ref, gate_up_ref, down_ref, out_ref, core_out, core_in, acc, wide_out, wide_in, thin_out, thin_in, hid, send_sems, recv_sems):
    me = lax.axis_index("pool")
    core, x, y = me % 2, me // 2 % 2, me // 4 % 2
    by_core, by_x, by_y = me + 1 - 2 * core, me + 2 - 4 * x, me + 4 - 8 * y
    units = acc.shape[1] // 2
    gate, up = pl.ds(0, units), pl.ds(units, units)
    fore, aft = pl.ds(0, units // 2), pl.ds(units // 2, units // 2)
    half = 4 * cap

    barrier = pltpu.get_barrier_semaphore()
    for partner in (by_core, by_x, by_y):
        pl.semaphore_signal(barrier, inc=1, device_id={"pool": partner}, device_id_type=pl.DeviceIdType.MESH)
    pl.semaphore_wait(barrier, 3)

    started = []

    def send(src, dst, partner):
        number = len(started)
        copy = pltpu.make_async_remote_copy(
            src_ref=src,
            dst_ref=dst,
            send_sem=send_sems.at[number],
            recv_sem=recv_sems.at[number],
            device_id={"pool": partner},
            device_id_type=pl.DeviceIdType.MESH,
        )
        copy.start()
        started.append(copy)
        return copy

    tile = units // 2
    crossing = []
    for side in (0, 1):

        @pl.loop(0, 2)
        def _(step, side=side):
            columns = pl.ds(pl.multiple_of(side * units + step * tile, tile), tile)
            core_out[:, columns] = jnp.dot(
                rows_ref[at(1 - core, half), :], gate_up_ref[:, columns], preferred_element_type=F32
            ).astype(BF)

        columns = (gate, up)[side]
        crossing.append(send(core_out.at[:, columns], core_in.at[:, columns], by_core))

    @pl.loop(0, 4)
    def _(step):
        columns = pl.ds(pl.multiple_of(step * tile, tile), tile)
        acc[:, columns] = jnp.dot(rows_ref[at(core, half), :], gate_up_ref[:, columns], preferred_element_type=F32)

    crossing[0].wait_recv()
    away = at(1 - x, 2 * cap)
    wide_out[0] = (acc[away, gate] + core_in[away, gate].astype(F32)).astype(BF)
    gate_one = send(wide_out.at[0], wide_in.at[0], by_x)
    crossing[1].wait_recv()
    for row in (0, 1):
        away = at(row * 2 + 1 - y, cap)
        wide_out[1, pl.ds(row * cap, cap), :] = (acc[away, up] + core_in[away, up].astype(F32)).astype(BF)
    up_one = send(wide_out.at[1], wide_in.at[1], by_y)

    gate_one.wait_recv()
    away = at(x * 2 + 1 - y, cap)
    thin_out[0] = (acc[away, gate] + core_in[away, gate].astype(F32) + wide_in[0, at(1 - y, cap), :].astype(F32)).astype(BF)
    gate_two = send(thin_out.at[0], thin_in.at[0], by_y)
    up_one.wait_recv()
    away = at((1 - x) * 2 + y, cap)
    thin_out[1] = (acc[away, up] + core_in[away, up].astype(F32) + wide_in[1, at(1 - x, cap), :].astype(F32)).astype(BF)
    up_two = send(thin_out.at[1], thin_in.at[1], by_x)

    home = at(x * 2 + y, cap)
    gate_two.wait_recv()
    gates = acc[home, gate] + core_in[home, gate].astype(F32) + wide_in[0, at(y, cap), :].astype(F32) + thin_in[0].astype(F32)
    gates = gates / (1.0 + jnp.exp(-gates))
    up_two.wait_recv()
    ups = acc[home, up] + core_in[home, up].astype(F32) + wide_in[1, at(x, cap), :].astype(F32) + thin_in[1].astype(F32)
    mine = at(core * 4 + x * 2 + y, cap)
    hid[mine, :] = (gates * ups).astype(BF)

    fore_y = send(hid.at[mine, fore], hid.at[mine, fore], by_y)
    aft_x = send(hid.at[mine, aft], hid.at[mine, aft], by_x)
    fore_x = send(hid.at[mine, fore], hid.at[mine, fore], by_x)
    aft_y = send(hid.at[mine, aft], hid.at[mine, aft], by_y)
    fore_y.wait_recv()
    theirs = at(core * 4 + x * 2 + 1 - y, cap)
    fore_on = send(hid.at[theirs, fore], hid.at[theirs, fore], by_x)
    aft_x.wait_recv()
    theirs = at(core * 4 + (1 - x) * 2 + y, cap)
    aft_on = send(hid.at[theirs, aft], hid.at[theirs, aft], by_y)
    for copy in (fore_x, aft_y, fore_on, aft_on):
        copy.wait_recv()
    mine = at(core, half)
    across = send(hid.at[mine, :], hid.at[mine, :], by_core)
    out_ref[mine, :] = jnp.dot(hid[mine, :], down_ref[...], preferred_element_type=F32).astype(BF)
    across.wait_recv()
    theirs = at(1 - core, half)
    out_ref[theirs, :] = jnp.dot(hid[theirs, :], down_ref[...], preferred_element_type=F32).astype(BF)
    for copy in started:
        copy.wait_send()


def expert(rows, gate_up, down):
    cap, units = rows.shape[0] // SPAN, down.shape[0]
    copies = 13
    flops = 2 * rows.shape[0] * rows.shape[1] * 3 * units
    return pl.pallas_call(
        functools.partial(expert_kernel, cap),
        out_shape=jax.ShapeDtypeStruct(rows.shape, BF),
        in_specs=[pl.BlockSpec(memory_space=pltpu.VMEM)] * 3,
        out_specs=pl.BlockSpec(memory_space=pltpu.VMEM),
        scratch_shapes=[
            pltpu.VMEM((4 * cap, 2 * units), BF),
            pltpu.VMEM((4 * cap, 2 * units), BF),
            pltpu.VMEM((4 * cap, 2 * units), F32),
            pltpu.VMEM((2, 2 * cap, units), BF),
            pltpu.VMEM((2, 2 * cap, units), BF),
            pltpu.VMEM((2, cap, units), BF),
            pltpu.VMEM((2, cap, units), BF),
            pltpu.VMEM((8 * cap, units), BF),
            pltpu.SemaphoreType.DMA((copies,)),
            pltpu.SemaphoreType.DMA((copies,)),
        ],
        compiler_params=pltpu.CompilerParams(collective_id=0, has_side_effects=True, vmem_limit_bytes=40 * 2**20),
        cost_estimate=pl.CostEstimate(flops=flops, bytes_accessed=40 * 2**20, transcendentals=0),
        name="expert",
    )(rows, gate_up, down)


def on_device(tokens, slot_ids, gate_codes, gate_up, down_proj):
    pool_size = lax.axis_size("pool")
    slots = pool_size // SPAN
    tok_rows, width = tokens.shape
    topk = slot_ids.shape[1]
    piece = width // SPAN
    capacity = min(tok_rows, 3 * tok_rows * topk // (2 * slots))
    capacity = -(-capacity // 16) * 16
    index = lax.axis_index("pool")
    own_slot = index // SPAN
    planes = [[s * SPAN + m for m in range(SPAN)] for s in range(slots)]

    routing = jnp.concatenate([slot_ids, gate_codes], axis=1)
    routing = lax.all_gather(routing, "pool", axis_index_groups=planes)
    plane_slots, plane_codes = routing[..., :topk], routing[..., topk:]
    pieces = tokens.reshape(tok_rows, SPAN, piece).transpose(1, 0, 2)
    plane_tokens = lax.all_to_all(pieces, "pool", split_axis=0, concat_axis=0, axis_index_groups=planes, tiled=True)

    def routes(slot):
        named = plane_slots == slot
        taken = jnp.any(named, axis=2)
        place = jnp.cumsum(taken.astype(jnp.int32), axis=1) - 1
        code = jnp.sum(jnp.where(named, plane_codes, 0), axis=2)
        hot = (place[:, :, None] == jnp.arange(capacity)) & taken[:, :, None]
        return hot, code

    blocks, mixers = [], []
    for step in range(slots):
        hot, code = routes(own_slot ^ step)
        high = jnp.where(hot, (code // 32)[:, :, None], 0).astype(F32) / 32.0
        low = jnp.where(hot, (code % 32)[:, :, None], 0).astype(F32) / 1024.0
        mixers.append((high.astype(BF), low.astype(BF)))
        block = jnp.einsum("jtc,jtd->jcd", hot.astype(BF), plane_tokens, preferred_element_type=F32)
        blocks.append(block.astype(BF).reshape(SPAN * capacity, piece))

    order = [0] + list(reversed(range(1, slots)))
    arrived = {step: swap(blocks[step], step * SPAN) if step else blocks[step] for step in order}
    mixed = jnp.zeros((SPAN, tok_rows, piece), F32)
    result = None
    for step in order:
        rows = arrived[step]
        if result is not None:
            rows, result = lax.optimization_barrier((rows, result))
        result = expert(rows, gate_up, down_proj)
        back = (swap(result, step * SPAN) if step else result).reshape(SPAN, capacity, piece)
        for part in mixers[step]:
            mixed = mixed + jnp.einsum("jtc,jcd->jtd", part, back, preferred_element_type=F32)
    out = lax.all_to_all(mixed.astype(BF), "pool", split_axis=0, concat_axis=0, axis_index_groups=planes, tiled=True)
    return out.transpose(1, 0, 2).reshape(tok_rows, width)


def solution(mesh):
    rows = P(("groups", "pool"), None)
    return jax.shard_map(
        on_device,
        mesh=mesh,
        in_specs=(rows, rows, rows, P("pool", None), P(None, "pool")),
        out_specs=rows,
        check_vma=False,
    )
```

```python
import functools
import jax
import jax.numpy as jnp
from jax import lax
from jax.experimental import pallas as pl
from jax.experimental.pallas import tpu as pltpu
from jax.sharding import PartitionSpec as P

SPAN = 8
BF = jnp.bfloat16
F32 = jnp.float32


def at(index, rows):
    return pl.ds(pl.multiple_of(index * rows, 16), rows)


done = object()


def expert_kernel(cap, slots, rows_ref, gate_up_ref, down_ref, out_ref, came, results, core_outs, core_ins, accs, wide_outs, wide_ins, thin_outs, thin_ins, hids, send_sems, recv_sems):
    me = lax.axis_index("pool")
    core, x, y = me % 2, me // 2 % 2, me // 4 % 2
    by_core, by_x, by_y = me + 1 - 2 * core, me + 2 - 4 * x, me + 4 - 8 * y
    units = accs.shape[2] // 2
    gate, up = pl.ds(0, units), pl.ds(units, units)
    fore, aft = pl.ds(0, units // 2), pl.ds(units // 2, units // 2)
    half = 4 * cap

    def across_slots(step):
        partner = me
        for bit in range(slots.bit_length() - 1):
            if step >> bit & 1:
                mask = SPAN << bit
                partner = partner + mask - 2 * mask * (me // mask % 2)
        return partner

    barrier = pltpu.get_barrier_semaphore()
    partners = [by_core, by_x, by_y] + [across_slots(step) for step in range(1, slots)]
    for partner in partners:
        pl.semaphore_signal(barrier, inc=1, device_id={"pool": partner}, device_id_type=pl.DeviceIdType.MESH)
    pl.semaphore_wait(barrier, len(partners))

    started = []
    used = [0] * slots

    def send_for(step, src, dst, partner):
        number = used[step]
        used[step] += 1
        copy = pltpu.make_async_remote_copy(
            src_ref=src,
            dst_ref=dst,
            send_sem=send_sems.at[step, number],
            recv_sem=recv_sems.at[step, number],
            device_id={"pool": partner},
            device_id_type=pl.DeviceIdType.MESH,
        )
        copy.start()
        started.append(copy)
        return copy

    inbound, outbound = {}, []

    def dispatch(step):
        inbound[step] = send_for(step, rows_ref.at[step], came.at[step - 1], across_slots(step))

    def block(step):
        send = functools.partial(send_for, step)
        core_out, core_in, acc, wide_out, wide_in, thin_out, thin_in, hid = (
            ref.at[step] for ref in (core_outs, core_ins, accs, wide_outs, wide_ins, thin_outs, thin_ins, hids)
        )
        rows, result = rows_ref.at[0], out_ref.at[0]
        if step:
            rows, result = came.at[step - 1], results.at[step - 1]
            inbound[step].wait_recv()
        tile = units // 2
        crossing = []
        for side in (0, 1):

            @pl.loop(0, 2)
            def _(step, side=side):
                columns = pl.ds(pl.multiple_of(side * units + step * tile, tile), tile)
                core_out[:, columns] = jnp.dot(
                    rows[at(1 - core, half), :], gate_up_ref[:, columns], preferred_element_type=F32
                ).astype(BF)

            columns = (gate, up)[side]
            crossing.append(send(core_out.at[:, columns], core_in.at[:, columns], by_core))

        @pl.loop(0, 4)
        def _(step):
            columns = pl.ds(pl.multiple_of(step * tile, tile), tile)
            acc[:, columns] = jnp.dot(rows[at(core, half), :], gate_up_ref[:, columns], preferred_element_type=F32)

        yield
        crossing[0].wait_recv()
        away = at(1 - x, 2 * cap)
        wide_out[0] = (acc[away, gate] + core_in[away, gate].astype(F32)).astype(BF)
        gate_one = send(wide_out.at[0], wide_in.at[0], by_x)
        yield
        crossing[1].wait_recv()
        for row in (0, 1):
            away = at(row * 2 + 1 - y, cap)
            wide_out[1, pl.ds(row * cap, cap), :] = (acc[away, up] + core_in[away, up].astype(F32)).astype(BF)
        up_one = send(wide_out.at[1], wide_in.at[1], by_y)

        yield
        gate_one.wait_recv()
        away = at(x * 2 + 1 - y, cap)
        thin_out[0] = (acc[away, gate] + core_in[away, gate].astype(F32) + wide_in[0, at(1 - y, cap), :].astype(F32)).astype(BF)
        gate_two = send(thin_out.at[0], thin_in.at[0], by_y)
        yield
        up_one.wait_recv()
        away = at((1 - x) * 2 + y, cap)
        thin_out[1] = (acc[away, up] + core_in[away, up].astype(F32) + wide_in[1, at(1 - x, cap), :].astype(F32)).astype(BF)
        up_two = send(thin_out.at[1], thin_in.at[1], by_x)

        home = at(x * 2 + y, cap)
        yield
        gate_two.wait_recv()
        gates = acc[home, gate] + core_in[home, gate].astype(F32) + wide_in[0, at(y, cap), :].astype(F32) + thin_in[0].astype(F32)
        gates = gates / (1.0 + jnp.exp(-gates))
        yield
        up_two.wait_recv()
        ups = acc[home, up] + core_in[home, up].astype(F32) + wide_in[1, at(x, cap), :].astype(F32) + thin_in[1].astype(F32)
        mine = at(core * 4 + x * 2 + y, cap)
        hid[mine, :] = (gates * ups).astype(BF)

        fore_y = send(hid.at[mine, fore], hid.at[mine, fore], by_y)
        aft_x = send(hid.at[mine, aft], hid.at[mine, aft], by_x)
        fore_x = send(hid.at[mine, fore], hid.at[mine, fore], by_x)
        aft_y = send(hid.at[mine, aft], hid.at[mine, aft], by_y)
        yield
        fore_y.wait_recv()
        theirs = at(core * 4 + x * 2 + 1 - y, cap)
        fore_on = send(hid.at[theirs, fore], hid.at[theirs, fore], by_x)
        yield
        aft_x.wait_recv()
        theirs = at(core * 4 + (1 - x) * 2 + y, cap)
        aft_on = send(hid.at[theirs, aft], hid.at[theirs, aft], by_y)
        yield
        for copy in (fore_x, aft_y, fore_on, aft_on):
            copy.wait_recv()
        mine = at(core, half)
        across = send(hid.at[mine, :], hid.at[mine, :], by_core)
        result[mine, :] = jnp.dot(hid[mine, :], down_ref[...], preferred_element_type=F32).astype(BF)
        yield
        across.wait_recv()
        theirs = at(1 - core, half)
        result[theirs, :] = jnp.dot(hid[theirs, :], down_ref[...], preferred_element_type=F32).astype(BF)

        if step:
            outbound.append(send(result, out_ref.at[step], across_slots(step)))

    order = list(reversed(range(1, slots)))
    if slots > 1:
        dispatch(order[0])
    for _ in block(0):
        pass
    for step in order[1:]:
        dispatch(step)
    for group in [order[:1]] + [order[first : first + 2] for first in range(1, len(order), 2)]:
        running = [block(step) for step in group]
        while running:
            running = [work for work in running if next(work, done) is not done]
    for copy in outbound:
        copy.wait_recv()
    for copy in started:
        copy.wait_send()


def experts(rows, gate_up, down):
    slots, cap, units = rows.shape[0], rows.shape[1] // SPAN, down.shape[0]
    copies = 15
    flops = 2 * rows.shape[0] * rows.shape[1] * rows.shape[2] * 3 * units
    return pl.pallas_call(
        functools.partial(expert_kernel, cap, slots),
        out_shape=jax.ShapeDtypeStruct(rows.shape, BF),
        in_specs=[pl.BlockSpec(memory_space=pltpu.VMEM)] * 3,
        out_specs=pl.BlockSpec(memory_space=pltpu.VMEM),
        scratch_shapes=[
            pltpu.VMEM((max(1, slots - 1),) + rows.shape[1:], BF),
            pltpu.VMEM((max(1, slots - 1),) + rows.shape[1:], BF),
            pltpu.VMEM((slots, 4 * cap, 2 * units), BF),
            pltpu.VMEM((slots, 4 * cap, 2 * units), BF),
            pltpu.VMEM((slots, 4 * cap, 2 * units), F32),
            pltpu.VMEM((slots, 2, 2 * cap, units), BF),
            pltpu.VMEM((slots, 2, 2 * cap, units), BF),
            pltpu.VMEM((slots, 2, cap, units), BF),
            pltpu.VMEM((slots, 2, cap, units), BF),
            pltpu.VMEM((slots, 8 * cap, units), BF),
            pltpu.SemaphoreType.DMA((slots, copies)),
            pltpu.SemaphoreType.DMA((slots, copies)),
        ],
        compiler_params=pltpu.CompilerParams(collective_id=0, has_side_effects=True, vmem_limit_bytes=60 * 2**20),
        cost_estimate=pl.CostEstimate(flops=flops, bytes_accessed=40 * 2**20, transcendentals=0),
        name="experts",
    )(rows, gate_up, down)


def on_device(tokens, slot_ids, gate_codes, gate_up, down_proj):
    pool_size = lax.axis_size("pool")
    slots = pool_size // SPAN
    tok_rows, width = tokens.shape
    topk = slot_ids.shape[1]
    piece = width // SPAN
    capacity = min(tok_rows, 3 * tok_rows * topk // (2 * slots))
    capacity = -(-capacity // 16) * 16
    index = lax.axis_index("pool")
    own_slot = index // SPAN
    planes = [[s * SPAN + m for m in range(SPAN)] for s in range(slots)]

    routing = jnp.concatenate([slot_ids, gate_codes], axis=1)
    routing = lax.all_gather(routing, "pool", axis_index_groups=planes)
    plane_slots, plane_codes = routing[..., :topk], routing[..., topk:]
    pieces = tokens.reshape(tok_rows, SPAN, piece).transpose(1, 0, 2)
    plane_tokens = lax.all_to_all(pieces, "pool", split_axis=0, concat_axis=0, axis_index_groups=planes, tiled=True)

    def routes(slot):
        named = plane_slots == slot
        taken = jnp.any(named, axis=2)
        place = jnp.cumsum(taken.astype(jnp.int32), axis=1) - 1
        code = jnp.sum(jnp.where(named, plane_codes, 0), axis=2)
        hot = (place[:, :, None] == jnp.arange(capacity)) & taken[:, :, None]
        return hot, code

    blocks, mixers = [], []
    for step in range(slots):
        hot, code = routes(own_slot ^ step)
        high = jnp.where(hot, (code // 32)[:, :, None], 0).astype(F32) / 32.0
        low = jnp.where(hot, (code % 32)[:, :, None], 0).astype(F32) / 1024.0
        mixers.append((high.astype(BF), low.astype(BF)))
        block = jnp.einsum("jtc,jtd->jcd", hot.astype(BF), plane_tokens, preferred_element_type=F32)
        blocks.append(block.astype(BF).reshape(SPAN * capacity, piece))

    returned = experts(jnp.stack(blocks), gate_up, down_proj)
    mixed = jnp.zeros((SPAN, tok_rows, piece), F32)
    for step in range(slots):
        back = returned[step].reshape(SPAN, capacity, piece)
        for part in mixers[step]:
            mixed = mixed + jnp.einsum("jtc,jcd->jtd", part, back, preferred_element_type=F32)
    out = lax.all_to_all(mixed.astype(BF), "pool", split_axis=0, concat_axis=0, axis_index_groups=planes, tiled=True)
    return out.transpose(1, 0, 2).reshape(tok_rows, width)


def solution(mesh):
    rows = P(("groups", "pool"), None)
    return jax.shard_map(
        on_device,
        mesh=mesh,
        in_specs=(rows, rows, rows, P("pool", None), P(None, "pool")),
        out_specs=rows,
        check_vma=False,
    )
```

```python
import functools
import jax
import jax.numpy as jnp
from jax import lax
from jax.experimental import pallas as pl
from jax.experimental.pallas import tpu as pltpu
from jax.sharding import PartitionSpec as P

SPAN = 8
BF = jnp.bfloat16
F32 = jnp.float32


def at(index, rows):
    return pl.ds(pl.multiple_of(index * rows, 16), rows)


done = object()


def expert_kernel(cap, slots, rows_ref, gate_up_ref, down_ref, out_ref, came, results, core_outs, core_ins, accs, wide_outs, wide_ins, thin_outs, thin_ins, hids, send_sems, recv_sems):
    me = lax.axis_index("pool")
    core, x, y = me % 2, me // 2 % 2, me // 4 % 2
    by_core, by_x, by_y = me + 1 - 2 * core, me + 2 - 4 * x, me + 4 - 8 * y
    units = accs.shape[2] // 2
    gate, up = pl.ds(0, units), pl.ds(units, units)
    fore, aft = pl.ds(0, units // 2), pl.ds(units // 2, units // 2)
    half = 4 * cap

    def across_slots(step):
        partner = me
        for bit in range(slots.bit_length() - 1):
            if step >> bit & 1:
                mask = SPAN << bit
                partner = partner + mask - 2 * mask * (me // mask % 2)
        return partner

    barrier = pltpu.get_barrier_semaphore()
    partners = [by_core, by_x, by_y] + [across_slots(step) for step in range(1, slots)]
    for partner in partners:
        pl.semaphore_signal(barrier, inc=1, device_id={"pool": partner}, device_id_type=pl.DeviceIdType.MESH)
    pl.semaphore_wait(barrier, len(partners))

    started = []
    used = [0] * slots

    def send_for(step, src, dst, partner):
        number = used[step]
        used[step] += 1
        copy = pltpu.make_async_remote_copy(
            src_ref=src,
            dst_ref=dst,
            send_sem=send_sems.at[step, number],
            recv_sem=recv_sems.at[step, number],
            device_id={"pool": partner},
            device_id_type=pl.DeviceIdType.MESH,
        )
        copy.start()
        started.append(copy)
        return copy

    inbound, outbound = {}, []

    def dispatch(step):
        inbound[step] = send_for(step, rows_ref.at[step], came.at[step - 1], across_slots(step))

    def block(step):
        send = functools.partial(send_for, step)
        core_out, core_in, acc, wide_out, wide_in, thin_out, thin_in, hid = (
            ref.at[step] for ref in (core_outs, core_ins, accs, wide_outs, wide_ins, thin_outs, thin_ins, hids)
        )
        rows, result = rows_ref.at[0], out_ref.at[0]
        if step:
            rows, result = came.at[step - 1], results.at[step - 1]
            inbound[step].wait_recv()
        tile = units // 2
        crossing = []
        for side in (0, 1):

            @pl.loop(0, 2)
            def _(step, side=side):
                columns = pl.ds(pl.multiple_of(side * units + step * tile, tile), tile)
                core_out[:, columns] = jnp.dot(
                    rows[at(1 - core, half), :], gate_up_ref[:, columns], preferred_element_type=F32
                ).astype(BF)

            columns = (gate, up)[side]
            crossing.append(send(core_out.at[:, columns], core_in.at[:, columns], by_core))

        @pl.loop(0, 4)
        def _(step):
            columns = pl.ds(pl.multiple_of(step * tile, tile), tile)
            acc[:, columns] = jnp.dot(rows[at(core, half), :], gate_up_ref[:, columns], preferred_element_type=F32)

        yield
        crossing[0].wait_recv()
        away = at(1 - x, 2 * cap)
        wide_out[0] = (acc[away, gate] + core_in[away, gate].astype(F32)).astype(BF)
        gate_one = send(wide_out.at[0], wide_in.at[0], by_x)
        yield
        crossing[1].wait_recv()
        for row in (0, 1):
            away = at(row * 2 + 1 - y, cap)
            wide_out[1, pl.ds(row * cap, cap), :] = (acc[away, up] + core_in[away, up].astype(F32)).astype(BF)
        up_one = send(wide_out.at[1], wide_in.at[1], by_y)

        yield
        gate_one.wait_recv()
        away = at(x * 2 + 1 - y, cap)
        thin_out[0] = (acc[away, gate] + core_in[away, gate].astype(F32) + wide_in[0, at(1 - y, cap), :].astype(F32)).astype(BF)
        gate_two = send(thin_out.at[0], thin_in.at[0], by_y)
        yield
        up_one.wait_recv()
        away = at((1 - x) * 2 + y, cap)
        thin_out[1] = (acc[away, up] + core_in[away, up].astype(F32) + wide_in[1, at(1 - x, cap), :].astype(F32)).astype(BF)
        up_two = send(thin_out.at[1], thin_in.at[1], by_x)

        home = at(x * 2 + y, cap)
        yield
        gate_two.wait_recv()
        gates = acc[home, gate] + core_in[home, gate].astype(F32) + wide_in[0, at(y, cap), :].astype(F32) + thin_in[0].astype(F32)
        gates = gates / (1.0 + jnp.exp(-gates))
        yield
        up_two.wait_recv()
        ups = acc[home, up] + core_in[home, up].astype(F32) + wide_in[1, at(x, cap), :].astype(F32) + thin_in[1].astype(F32)
        mine = at(core * 4 + x * 2 + y, cap)
        hid[mine, :] = (gates * ups).astype(BF)

        fore_y = send(hid.at[mine, fore], hid.at[mine, fore], by_y)
        aft_x = send(hid.at[mine, aft], hid.at[mine, aft], by_x)
        fore_x = send(hid.at[mine, fore], hid.at[mine, fore], by_x)
        aft_y = send(hid.at[mine, aft], hid.at[mine, aft], by_y)
        yield
        fore_y.wait_recv()
        theirs = at(core * 4 + x * 2 + 1 - y, cap)
        fore_on = send(hid.at[theirs, fore], hid.at[theirs, fore], by_x)
        yield
        aft_x.wait_recv()
        theirs = at(core * 4 + (1 - x) * 2 + y, cap)
        aft_on = send(hid.at[theirs, aft], hid.at[theirs, aft], by_y)
        yield
        for copy in (fore_x, aft_y, fore_on, aft_on):
            copy.wait_recv()
        mine = at(core, half)
        across = send(hid.at[mine, :], hid.at[mine, :], by_core)
        result[mine, :] = jnp.dot(hid[mine, :], down_ref[...], preferred_element_type=F32).astype(BF)
        yield
        across.wait_recv()
        theirs = at(1 - core, half)
        result[theirs, :] = jnp.dot(hid[theirs, :], down_ref[...], preferred_element_type=F32).astype(BF)

        if step:
            outbound.append(send(result, out_ref.at[step], across_slots(step)))

    order = list(reversed(range(1, slots)))
    for step in order[1:]:
        dispatch(step)
    for _ in block(0):
        pass
    dispatch(order[0])
    order = order[1:] + order[:1]
    for group in [order[first : first + 2] for first in range(0, len(order), 2)]:
        running = [block(step) for step in group]
        while running:
            running = [work for work in running if next(work, done) is not done]
    for copy in outbound:
        copy.wait_recv()
    for copy in started:
        copy.wait_send()


def experts(rows, gate_up, down):
    slots, cap, units = rows.shape[0], rows.shape[1] // SPAN, down.shape[0]
    copies = 15
    flops = 2 * rows.shape[0] * rows.shape[1] * rows.shape[2] * 3 * units
    return pl.pallas_call(
        functools.partial(expert_kernel, cap, slots),
        out_shape=jax.ShapeDtypeStruct(rows.shape, BF),
        in_specs=[pl.BlockSpec(memory_space=pltpu.VMEM)] * 3,
        out_specs=pl.BlockSpec(memory_space=pltpu.VMEM),
        scratch_shapes=[
            pltpu.VMEM((max(1, slots - 1),) + rows.shape[1:], BF),
            pltpu.VMEM((max(1, slots - 1),) + rows.shape[1:], BF),
            pltpu.VMEM((slots, 4 * cap, 2 * units), BF),
            pltpu.VMEM((slots, 4 * cap, 2 * units), BF),
            pltpu.VMEM((slots, 4 * cap, 2 * units), F32),
            pltpu.VMEM((slots, 2, 2 * cap, units), BF),
            pltpu.VMEM((slots, 2, 2 * cap, units), BF),
            pltpu.VMEM((slots, 2, cap, units), BF),
            pltpu.VMEM((slots, 2, cap, units), BF),
            pltpu.VMEM((slots, 8 * cap, units), BF),
            pltpu.SemaphoreType.DMA((slots, copies)),
            pltpu.SemaphoreType.DMA((slots, copies)),
        ],
        compiler_params=pltpu.CompilerParams(collective_id=0, has_side_effects=True, vmem_limit_bytes=60 * 2**20),
        cost_estimate=pl.CostEstimate(flops=flops, bytes_accessed=40 * 2**20, transcendentals=0),
        name="experts",
    )(rows, gate_up, down)


def on_device(tokens, slot_ids, gate_codes, gate_up, down_proj):
    pool_size = lax.axis_size("pool")
    slots = pool_size // SPAN
    tok_rows, width = tokens.shape
    topk = slot_ids.shape[1]
    piece = width // SPAN
    capacity = min(tok_rows, 3 * tok_rows * topk // (2 * slots))
    capacity = -(-capacity // 16) * 16
    index = lax.axis_index("pool")
    own_slot = index // SPAN
    planes = [[s * SPAN + m for m in range(SPAN)] for s in range(slots)]

    routing = jnp.concatenate([slot_ids, gate_codes], axis=1)
    routing = lax.all_gather(routing, "pool", axis_index_groups=planes)
    plane_slots, plane_codes = routing[..., :topk], routing[..., topk:]
    pieces = tokens.reshape(tok_rows, SPAN, piece).transpose(1, 0, 2)
    plane_tokens = lax.all_to_all(pieces, "pool", split_axis=0, concat_axis=0, axis_index_groups=planes, tiled=True)

    def routes(slot):
        named = plane_slots == slot
        taken = jnp.any(named, axis=2)
        place = jnp.cumsum(taken.astype(jnp.int32), axis=1) - 1
        code = jnp.sum(jnp.where(named, plane_codes, 0), axis=2)
        hot = (place[:, :, None] == jnp.arange(capacity)) & taken[:, :, None]
        return hot, code

    blocks, mixers = [], []
    for step in range(slots):
        hot, code = routes(own_slot ^ step)
        high = jnp.where(hot, (code // 32)[:, :, None], 0).astype(F32) / 32.0
        low = jnp.where(hot, (code % 32)[:, :, None], 0).astype(F32) / 1024.0
        mixers.append((high.astype(BF), low.astype(BF)))
        block = jnp.einsum("jtc,jtd->jcd", hot.astype(BF), plane_tokens, preferred_element_type=F32)
        blocks.append(block.astype(BF).reshape(SPAN * capacity, piece))

    returned = experts(jnp.stack(blocks), gate_up, down_proj)
    mixed = jnp.zeros((SPAN, tok_rows, piece), F32)
    for step in range(slots):
        back = returned[step].reshape(SPAN, capacity, piece)
        for part in mixers[step]:
            mixed = mixed + jnp.einsum("jtc,jcd->jtd", part, back, preferred_element_type=F32)
    out = lax.all_to_all(mixed.astype(BF), "pool", split_axis=0, concat_axis=0, axis_index_groups=planes, tiled=True)
    return out.transpose(1, 0, 2).reshape(tok_rows, width)


def solution(mesh):
    rows = P(("groups", "pool"), None)
    return jax.shard_map(
        on_device,
        mesh=mesh,
        in_specs=(rows, rows, rows, P("pool", None), P(None, "pool")),
        out_specs=rows,
        check_vma=False,
    )
```

```python
import functools
import jax
import jax.numpy as jnp
from jax import lax
from jax.experimental import pallas as pl
from jax.experimental.pallas import tpu as pltpu
from jax.sharding import PartitionSpec as P

SPAN = 8
BF = jnp.bfloat16
F32 = jnp.float32


def at(index, rows):
    return pl.ds(pl.multiple_of(index * rows, 16), rows)


done = object()


def expert_kernel(cap, slots, *refs):
    rows_refs = refs[:slots]
    (gate_up_ref, down_ref, out_ref, came, results, core_outs, core_ins, accs, wide_outs, wide_ins, thin_outs, thin_ins, hids, send_sems, recv_sems) = refs[slots:]
    me = lax.axis_index("pool")
    core, x, y = me % 2, me // 2 % 2, me // 4 % 2
    by_core, by_x, by_y = me + 1 - 2 * core, me + 2 - 4 * x, me + 4 - 8 * y
    units = accs.shape[2] // 2
    gate, up = pl.ds(0, units), pl.ds(units, units)
    fore, aft = pl.ds(0, units // 2), pl.ds(units // 2, units // 2)
    half = 4 * cap

    def across_slots(step):
        partner = me
        for bit in range(slots.bit_length() - 1):
            if step >> bit & 1:
                mask = SPAN << bit
                partner = partner + mask - 2 * mask * (me // mask % 2)
        return partner

    barrier = pltpu.get_barrier_semaphore()
    partners = [by_core, by_x, by_y] + [across_slots(step) for step in range(1, slots)]
    for partner in partners:
        pl.semaphore_signal(barrier, inc=1, device_id={"pool": partner}, device_id_type=pl.DeviceIdType.MESH)
    pl.semaphore_wait(barrier, len(partners))

    started = []
    used = [0] * slots

    def send_for(step, src, dst, partner):
        number = used[step]
        used[step] += 1
        copy = pltpu.make_async_remote_copy(
            src_ref=src,
            dst_ref=dst,
            send_sem=send_sems.at[step, number],
            recv_sem=recv_sems.at[step, number],
            device_id={"pool": partner},
            device_id_type=pl.DeviceIdType.MESH,
        )
        copy.start()
        started.append(copy)
        return copy

    inbound, outbound = {}, []

    def dispatch(step):
        inbound[step] = send_for(step, rows_refs[step], came.at[step - 1], across_slots(step))

    def block(step):
        send = functools.partial(send_for, step)
        core_out, core_in, acc, wide_out, wide_in, thin_out, thin_in, hid = (
            ref.at[step] for ref in (core_outs, core_ins, accs, wide_outs, wide_ins, thin_outs, thin_ins, hids)
        )
        rows, result = rows_refs[0], out_ref.at[0]
        if step:
            rows, result = came.at[step - 1], results.at[step - 1]
            inbound[step].wait_recv()
        tile = units // 2
        crossing = []
        for side in (0, 1):

            @pl.loop(0, 2)
            def _(step, side=side):
                columns = pl.ds(pl.multiple_of(side * units + step * tile, tile), tile)
                core_out[:, columns] = jnp.dot(
                    rows[at(1 - core, half), :], gate_up_ref[:, columns], preferred_element_type=F32
                ).astype(BF)

            columns = (gate, up)[side]
            crossing.append(send(core_out.at[:, columns], core_in.at[:, columns], by_core))

        @pl.loop(0, 4)
        def _(step):
            columns = pl.ds(pl.multiple_of(step * tile, tile), tile)
            acc[:, columns] = jnp.dot(rows[at(core, half), :], gate_up_ref[:, columns], preferred_element_type=F32)

        yield
        crossing[0].wait_recv()
        away = at(1 - x, 2 * cap)
        wide_out[0] = (acc[away, gate] + core_in[away, gate].astype(F32)).astype(BF)
        gate_one = send(wide_out.at[0], wide_in.at[0], by_x)
        yield
        crossing[1].wait_recv()
        for row in (0, 1):
            away = at(row * 2 + 1 - y, cap)
            wide_out[1, pl.ds(row * cap, cap), :] = (acc[away, up] + core_in[away, up].astype(F32)).astype(BF)
        up_one = send(wide_out.at[1], wide_in.at[1], by_y)

        yield
        gate_one.wait_recv()
        away = at(x * 2 + 1 - y, cap)
        thin_out[0] = (acc[away, gate] + core_in[away, gate].astype(F32) + wide_in[0, at(1 - y, cap), :].astype(F32)).astype(BF)
        gate_two = send(thin_out.at[0], thin_in.at[0], by_y)
        yield
        up_one.wait_recv()
        away = at((1 - x) * 2 + y, cap)
        thin_out[1] = (acc[away, up] + core_in[away, up].astype(F32) + wide_in[1, at(1 - x, cap), :].astype(F32)).astype(BF)
        up_two = send(thin_out.at[1], thin_in.at[1], by_x)

        home = at(x * 2 + y, cap)
        yield
        gate_two.wait_recv()
        gates = acc[home, gate] + core_in[home, gate].astype(F32) + wide_in[0, at(y, cap), :].astype(F32) + thin_in[0].astype(F32)
        gates = gates / (1.0 + jnp.exp(-gates))
        yield
        up_two.wait_recv()
        ups = acc[home, up] + core_in[home, up].astype(F32) + wide_in[1, at(x, cap), :].astype(F32) + thin_in[1].astype(F32)
        mine = at(core * 4 + x * 2 + y, cap)
        hid[mine, :] = (gates * ups).astype(BF)

        fore_y = send(hid.at[mine, fore], hid.at[mine, fore], by_y)
        aft_x = send(hid.at[mine, aft], hid.at[mine, aft], by_x)
        fore_x = send(hid.at[mine, fore], hid.at[mine, fore], by_x)
        aft_y = send(hid.at[mine, aft], hid.at[mine, aft], by_y)
        yield
        fore_y.wait_recv()
        theirs = at(core * 4 + x * 2 + 1 - y, cap)
        fore_on = send(hid.at[theirs, fore], hid.at[theirs, fore], by_x)
        yield
        aft_x.wait_recv()
        theirs = at(core * 4 + (1 - x) * 2 + y, cap)
        aft_on = send(hid.at[theirs, aft], hid.at[theirs, aft], by_y)
        yield
        for copy in (fore_x, aft_y, fore_on, aft_on):
            copy.wait_recv()
        mine = at(core, half)
        across = send(hid.at[mine, :], hid.at[mine, :], by_core)
        result[mine, :] = jnp.dot(hid[mine, :], down_ref[...], preferred_element_type=F32).astype(BF)
        yield
        across.wait_recv()
        theirs = at(1 - core, half)
        result[theirs, :] = jnp.dot(hid[theirs, :], down_ref[...], preferred_element_type=F32).astype(BF)

        if step:
            outbound.append(send(result, out_ref.at[step], across_slots(step)))

    order = list(reversed(range(1, slots)))
    for step in order[1:]:
        dispatch(step)
    for _ in block(0):
        pass
    dispatch(order[0])
    order = order[1:] + order[:1]
    for group in [order[first : first + 2] for first in range(0, len(order), 2)]:
        running = [block(step) for step in group]
        while running:
            running = [work for work in running if next(work, done) is not done]
    for copy in outbound:
        copy.wait_recv()
    for copy in started:
        copy.wait_send()


def experts(blocks, gate_up, down):
    slots, cap, units = len(blocks), blocks[0].shape[0] // SPAN, down.shape[0]
    shape = (slots,) + blocks[0].shape
    copies = 15
    flops = 2 * shape[0] * shape[1] * shape[2] * 3 * units
    return pl.pallas_call(
        functools.partial(expert_kernel, cap, slots),
        out_shape=jax.ShapeDtypeStruct(shape, BF),
        in_specs=[pl.BlockSpec(memory_space=pltpu.VMEM)] * (slots + 2),
        out_specs=pl.BlockSpec(memory_space=pltpu.VMEM),
        scratch_shapes=[
            pltpu.VMEM((max(1, slots - 1),) + shape[1:], BF),
            pltpu.VMEM((max(1, slots - 1),) + shape[1:], BF),
            pltpu.VMEM((slots, 4 * cap, 2 * units), BF),
            pltpu.VMEM((slots, 4 * cap, 2 * units), BF),
            pltpu.VMEM((slots, 4 * cap, 2 * units), F32),
            pltpu.VMEM((slots, 2, 2 * cap, units), BF),
            pltpu.VMEM((slots, 2, 2 * cap, units), BF),
            pltpu.VMEM((slots, 2, cap, units), BF),
            pltpu.VMEM((slots, 2, cap, units), BF),
            pltpu.VMEM((slots, 8 * cap, units), BF),
            pltpu.SemaphoreType.DMA((slots, copies)),
            pltpu.SemaphoreType.DMA((slots, copies)),
        ],
        compiler_params=pltpu.CompilerParams(collective_id=0, has_side_effects=True, vmem_limit_bytes=60 * 2**20),
        cost_estimate=pl.CostEstimate(flops=flops, bytes_accessed=40 * 2**20, transcendentals=0),
        name="experts",
    )(*blocks, gate_up, down)


def on_device(tokens, slot_ids, gate_codes, gate_up, down_proj):
    pool_size = lax.axis_size("pool")
    slots = pool_size // SPAN
    tok_rows, width = tokens.shape
    topk = slot_ids.shape[1]
    piece = width // SPAN
    capacity = min(tok_rows, 3 * tok_rows * topk // (2 * slots))
    capacity = -(-capacity // 16) * 16
    index = lax.axis_index("pool")
    own_slot = index // SPAN
    planes = [[s * SPAN + m for m in range(SPAN)] for s in range(slots)]

    routing = jnp.concatenate([slot_ids, gate_codes], axis=1)
    routing = lax.all_gather(routing, "pool", axis_index_groups=planes)
    plane_slots, plane_codes = routing[..., :topk], routing[..., topk:]
    pieces = tokens.reshape(tok_rows, SPAN, piece).transpose(1, 0, 2)
    plane_tokens = lax.all_to_all(pieces, "pool", split_axis=0, concat_axis=0, axis_index_groups=planes, tiled=True)

    def routes(slot):
        named = plane_slots == slot
        taken = jnp.any(named, axis=2)
        place = jnp.cumsum(taken.astype(jnp.int32), axis=1) - 1
        code = jnp.sum(jnp.where(named, plane_codes, 0), axis=2)
        hot = (place[:, :, None] == jnp.arange(capacity)) & taken[:, :, None]
        return hot, code

    blocks, mixers = [], []
    for step in range(slots):
        hot, code = routes(own_slot ^ step)
        high = jnp.where(hot, (code // 32)[:, :, None], 0).astype(F32) / 32.0
        low = jnp.where(hot, (code % 32)[:, :, None], 0).astype(F32) / 1024.0
        mixers.append((high.astype(BF), low.astype(BF)))
        block = jnp.einsum("jtc,jtd->jcd", hot.astype(BF), plane_tokens, preferred_element_type=F32)
        blocks.append(block.astype(BF).reshape(SPAN * capacity, piece))

    returned = experts(blocks, gate_up, down_proj)
    mixed = jnp.zeros((SPAN, tok_rows, piece), F32)
    for step in range(slots):
        back = returned[step].reshape(SPAN, capacity, piece)
        for part in mixers[step]:
            mixed = mixed + jnp.einsum("jtc,jcd->jtd", part, back, preferred_element_type=F32)
    out = lax.all_to_all(mixed.astype(BF), "pool", split_axis=0, concat_axis=0, axis_index_groups=planes, tiled=True)
    return out.transpose(1, 0, 2).reshape(tok_rows, width)


def solution(mesh):
    rows = P(("groups", "pool"), None)
    return jax.shard_map(
        on_device,
        mesh=mesh,
        in_specs=(rows, rows, rows, P("pool", None), P(None, "pool")),
        out_specs=rows,
        check_vma=False,
    )
```
